256 devices in a mesh: row: 32 (over x, y, core), col: 8 (over z).
Axes of the slice: x: 4, y: 4, z: 8, core: 2. Of those that a mesh axis runs over, the one named last changes fastest.
Arguments:
- features: bfloat16 [262144, 128], P(('row', 'col')), may hold values from -6 to 6
- adjacency: bfloat16 [32, 8, 64, 256, 256], P('row', 'col'), as said below
- block_rows: int32 [32, 8, 64], P('row', 'col'), may hold values from 0 to 31
- block_cols: int32 [32, 8, 64], P('row', 'col'), may hold values from 0 to 127
- live_counts: int32 [32, 8], P('row', 'col'), may hold values from 8 to 64, as said below
- self_weight: bfloat16 [128, 256], replicated, may hold values from -0.5 to 0.5
- neigh_weight: bfloat16 [128, 256], replicated, may hold values from -4 to 4
- out_bias: float32 [256], replicated, may hold values from -3 to 3
Outputs:
- hidden_out: bfloat16 [262144, 256], P(('row', 'col'))
The draws below stay inside these ranges and needn't reach their ends.
Inputs may be any that keep to these rules, and one draw needn't show every extreme that they name: `live_counts`: every tile has between 8 and 64 live slots; some tile has exactly 64 and some tile exactly 8. Slots at or past the count hold arbitrary blocks and indices. `adjacency`: entries are zero or positive.
All inputs are finite; a program needn't handle non-finite values.
Results may differ from the reference program's by a relative error of at most 0.0033.
Values may be sent and summed in bfloat16 or wider, within the bound.
A program may use at most 128 MiB of HBM per device.

```python
import jax
import jax.numpy as jnp
from jax import lax

FEAT = 128
HID = 256
BLK = 256
ROWS_DEV = 1024
MAXB = 64
RB = 32
CB = 128
NODES = 262144
N_ROW = 32
N_COL = 8


def draw_adjacency(key, part):
    key = jax.random.fold_in(key, 7)
    first_key, second_key = jax.random.split(key)
    shape = (N_ROW, N_COL, MAXB, BLK, BLK)
    present = jax.random.bernoulli(first_key, 0.125, shape).astype(jnp.float32)
    values = jax.random.uniform(second_key, shape, jnp.float32, 0.5, 1.5)
    return (present * values).astype(jnp.bfloat16)


def draw_live_counts(key, part):
    key = jax.random.fold_in(key, 11)
    key_one, key_two, key_three = jax.random.split(key, 3)
    total = N_ROW * N_COL
    powers = jax.random.randint(key_one, (total,), 0, 4)
    counts = jnp.right_shift(jnp.full((total,), MAXB, jnp.int32), powers.astype(jnp.int32))
    first = jax.random.randint(key_two, (), 0, total)
    second = (first + 1 + jax.random.randint(key_three, (), 0, total - 1)) % total
    counts = counts.at[first].set(MAXB).at[second].set(MAXB // 8)
    return counts.reshape(N_ROW, N_COL).astype(jnp.int32)


def place_ends(result, key, smallest, high):
    dims = result.shape
    place = [jax.random.randint(jax.random.fold_in(key, axis), (), 0, dims[axis]) for axis in range(len(dims))]
    result = result.at[tuple(place)].set(smallest)
    longest = dims.index(max(dims))
    place[longest] = (place[longest] + 1) % dims[longest]
    return result.at[tuple(place)].set(high)


def level_of(rng, extent, cuts, least, top_value):
    factor_of = 1.0
    for dim, parts in cuts:
        steps = jax.random.uniform(jax.random.fold_in(jax.random.fold_in(rng, 6), dim), (parts,), jnp.float32, least / len(cuts), top_value / len(cuts))
        factor_of = factor_of * jnp.repeat(jnp.exp(steps), extent[dim] // parts).reshape((-1,) + (1,) * (len(extent) - 1 - dim))
    return factor_of


def scatter_about(rng, dims, width, bound, cuts=(), dtype=jnp.bfloat16):
    values = width * jax.random.normal(rng, dims, jnp.float32)
    if cuts:
        values = values * level_of(rng, dims, cuts, -0.22, 0.18)
    return jnp.clip(values, -bound, bound).astype(dtype)


def setup_inputs(seed: int = 0) -> dict:
    arg_keys = jax.random.split(jax.random.key(seed), 9)
    features = scatter_about(arg_keys[0], (NODES, FEAT), 1.0, 6.0, ((0, 256),))
    adjacency = draw_adjacency(jax.random.fold_in(arg_keys[8], 71), 0)
    block_rows = place_ends(jax.random.randint(arg_keys[2], (N_ROW, N_COL, MAXB), 0, RB), jax.random.fold_in(arg_keys[2], 1), 0, RB - 1).astype(jnp.int32)
    block_cols = place_ends(jax.random.randint(arg_keys[3], (N_ROW, N_COL, MAXB), 0, CB), jax.random.fold_in(arg_keys[3], 1), 0, CB - 1).astype(jnp.int32)
    live_counts = draw_live_counts(jax.random.fold_in(arg_keys[8], 71), 0)
    self_weight = scatter_about(arg_keys[5], (FEAT, HID), FEAT ** -0.5, 0.5)
    neigh_weight = scatter_about(arg_keys[6], (FEAT, HID), 0.7, 4.0)
    out_bias = scatter_about(arg_keys[7], (HID,), 0.5, 3.0, (), jnp.float32)
    return {"features": features, "adjacency": adjacency, "block_rows": block_rows, "block_cols": block_cols, "live_counts": live_counts, "self_weight": self_weight, "neigh_weight": neigh_weight, "out_bias": out_bias}


def reference(features, adjacency, block_rows, block_cols, live_counts, self_weight, neigh_weight, out_bias):
    row_blocks = N_COL * ROWS_DEV // BLK
    col_blocks = N_ROW * ROWS_DEV // BLK
    grid = features.reshape(N_ROW, N_COL, ROWS_DEV, FEAT)

    def one_row(index):
        tiles = adjacency[index]
        rows_here = block_rows[index]
        cols_here = block_cols[index]
        counts_here = live_counts[index]

        def one_tile(colidx):
            tile = tiles[colidx]
            column_x = jnp.take(grid, colidx, axis=1).reshape(col_blocks, BLK, FEAT)
            picked = column_x[cols_here[colidx]]
            products = jnp.einsum("sij,sjf->sif", tile.astype(jnp.float32), picked.astype(jnp.float32))
            valid = jnp.arange(MAXB) < counts_here[colidx]
            target = jnp.where(valid, rows_here[colidx], row_blocks).astype(jnp.int32)
            partial_value = jnp.zeros((row_blocks + 1, BLK, FEAT), jnp.float32).at[target].add(products)[:row_blocks]
            row_weight = jnp.sum(tile.astype(jnp.float32), axis=-1)
            weights = jnp.zeros((row_blocks + 1, BLK), jnp.float32).at[target].add(row_weight)[:row_blocks]
            return partial_value, weights

        partials, weights = lax.map(one_tile, jnp.arange(N_COL))
        summed = jnp.sum(partials, axis=0).reshape(row_blocks * BLK, FEAT)
        degree = 1.0 + jnp.sum(weights, axis=0).reshape(row_blocks * BLK)
        neigh_mean = (summed / degree[:, None]).astype(jnp.bfloat16)
        own = grid[index].reshape(N_COL * ROWS_DEV, FEAT)
        total = jnp.dot(own, self_weight, preferred_element_type=jnp.float32)
        total = total + jnp.dot(neigh_mean, neigh_weight, preferred_element_type=jnp.float32) + out_bias
        return jax.nn.relu(total).astype(jnp.bfloat16)

    stacked = lax.map(one_row, jnp.arange(N_ROW))
    return stacked.reshape(NODES, HID)
```

```python
import jax
import jax.numpy as jnp
from jax import lax
from jax.sharding import PartitionSpec as P


def per_device(
    features, adjacency, block_rows, block_cols, live_counts, self_weight, neigh_weight, out_bias
):
    rows_dev, feat = features.shape
    block = adjacency.shape[-1]
    slots = adjacency.shape[2]
    ncols = lax.axis_size("col")
    nrows = lax.axis_size("row")
    row_blocks = ncols * rows_dev // block
    col_blocks = nrows * rows_dev // block
    tile = adjacency[0, 0]
    rows_here = block_rows[0, 0]
    cols_here = block_cols[0, 0]
    count = live_counts[0, 0]
    column_x = lax.all_gather(features, "row", axis=0, tiled=True)
    picked = column_x.reshape(col_blocks, block, feat)[cols_here]
    products = jnp.einsum("sij,sjf->sif", tile, picked, preferred_element_type=jnp.float32)
    valid = jnp.arange(slots) < count
    target = jnp.where(valid, rows_here, row_blocks)
    partial_value = (
        jnp.zeros((row_blocks + 1, block, feat), jnp.float32).at[target].add(products)[:row_blocks]
    )
    partial_value = partial_value.reshape(row_blocks * block, feat)
    row_weight = jnp.sum(tile, axis=-1, dtype=jnp.float32)
    weights = (
        jnp.zeros((row_blocks + 1, block), jnp.float32).at[target].add(row_weight)[:row_blocks]
    )
    weights = weights.reshape(row_blocks * block)
    summed = lax.psum_scatter(partial_value, "col", scatter_dimension=0, tiled=True)
    degree = lax.psum_scatter(weights, "col", scatter_dimension=0, tiled=True)
    neigh_mean = (summed / (1.0 + degree)[:, None]).astype(jnp.bfloat16)
    total = jnp.dot(features, self_weight, preferred_element_type=jnp.float32)
    total = total + jnp.dot(neigh_mean, neigh_weight, preferred_element_type=jnp.float32) + out_bias
    return jax.nn.relu(total).astype(jnp.bfloat16)


def solution(mesh):
    in_specs = (
        P(("row", "col"), None),
        P("row", "col", None, None, None),
        P("row", "col", None),
        P("row", "col", None),
        P("row", "col"),
        P(),
        P(),
        P(),
    )
    out_specs = P(("row", "col"), None)
    return jax.shard_map(
        per_device, mesh=mesh, in_specs=in_specs, out_specs=out_specs, check_vma=False
    )
```

```python
import functools

import jax
import jax.numpy as jnp
from jax import lax
from jax.experimental import pallas as pl
from jax.experimental.pallas import tpu as pltpu
from jax.sharding import PartitionSpec as P

MESH = pl.DeviceIdType.MESH
F32, BF16 = jnp.float32, jnp.bfloat16

SIDE = 4
NZ = 8
BLK = 256
FEAT = 128
HID = 256
SLOTS = 64
DEST = 4
CHUNKS = 4
FC = FEAT // CHUNKS
GROUP = 16
UNROLL = 8
ONES = 16

COL, PREV, LAST = 0, SLOTS, 2 * SLOTS

N_GATHER = 13


def nt(a, b):
    return lax.dot_general(a, b, (((1,), (1,)), ((), ())), preferred_element_type=F32)


def tn(a, b):
    return lax.dot_general(a, b, (((0,), (0,)), ((), ())), preferred_element_type=F32)


def layer_kernel(
    plan,
    x_ref,
    adj_hbm,
    ws_ref,
    wn_ref,
    bias_ref,
    out_ref,
    *scratch,
):
    held = scratch[:CHUNKS]
    (
        tiles,
        sums,
        degs,
        rs_send,
        rs_recv,
        deg_send,
        deg_recv,
        mean_t,
        tile_sem,
        g_send,
        g_recv,
        r_send,
        r_recv,
        d_send,
        d_recv,
    ) = scratch[CHUNKS:]

    row, z = lax.axis_index("row"), lax.axis_index("col")
    k = row % 2
    cx, cy = row // (2 * SIDE), (row // 2) % SIDE
    i = (1 - k) * cx + k * cy
    j = (1 - k) * cy + k * cx

    def device(ii, jj):
        return (ii * (8 - 6 * k) + jj * (2 + 6 * k) + k, z)

    def place(kk, jj, ii):
        return kk * 16 + jj * 4 + ii

    ip, im, i2 = (i + 1) % SIDE, (i + 3) % SIDE, (i + 2) % SIDE
    jp, jm, j2 = (j + 1) % SIDE, (j + 3) % SIDE, (j + 2) % SIDE
    a_plus, a_minus = device(ip, j), device(im, j)
    b_plus, b_minus = device(i, jp), device(i, jm)
    sibling = (row + 1 - 2 * k, z)
    z_plus, z_minus = (row, (z + 1) % NZ), (row, (z + NZ - 1) % NZ)

    barrier = pltpu.get_barrier_semaphore()
    for peer in (a_plus, a_minus, b_plus, b_minus, sibling):
        pl.semaphore_signal(barrier, inc=1, device_id=peer, device_id_type=MESH)
    for off in range(1, NZ):
        pl.semaphore_signal(
            barrier, inc=1, device_id=(row, (z + off) % NZ), device_id_type=MESH
        )

    load = pltpu.make_async_copy(adj_hbm.at[0, 0], tiles, tile_sem)
    load.start()

    mine = place(k, j, i)
    for c in range(CHUNKS):
        eye = (
            lax.broadcasted_iota(jnp.int32, (FC, FEAT), 0) + c * FC
            == lax.broadcasted_iota(jnp.int32, (FC, FEAT), 1)
        ).astype(F32).astype(BF16)
        for b in range(DEST):
            held[c][mine, b] = nt(eye, x_ref[b * BLK : (b + 1) * BLK, :]).astype(BF16)

    sums[0, SLOTS] = jnp.zeros((FC, BLK), F32)
    sums[1, SLOTS] = jnp.zeros((FC, BLK), F32)
    degs[SLOTS] = jnp.zeros((8, BLK), F32)

    pl.semaphore_wait(barrier, 5 + NZ - 1)

    sent = []

    def send(c, n, ref, to):
        copy = pltpu.make_async_remote_copy(
            src_ref=ref,
            dst_ref=ref,
            send_sem=g_send.at[c, n],
            recv_sem=g_recv.at[c, n],
            device_id=to,
            device_id_type=MESH,
        )
        copy.start()
        sent.append(copy)

    def got(c, n, ref):
        pltpu.make_async_remote_copy(
            src_ref=ref,
            dst_ref=ref,
            send_sem=g_send.at[c, n],
            recv_sem=g_recv.at[c, n],
            device_id=sibling,
            device_id_type=MESH,
        ).wait_recv()

    def block(c, ii):
        return held[c].at[place(k, j, ii)]

    def block_half(c, ii, h):
        return held[c].at[place(k, j, ii), pl.ds(2 * h, 2)]

    def line(c, jj, kk=None):
        return held[c].at[pl.ds(place(k if kk is None else kk, jj, 0), 4)]

    def line_half(c, jj, h, kk=None):
        return held[c].at[pl.ds(place(k if kk is None else kk, jj, 2 * h), 2)]

    def first_axis_own(c):
        send(c, 0, block(c, i), a_plus)
        send(c, 1, block(c, i), a_minus)

    def first_axis_forward(c):
        got(c, 0, block(c, im))
        send(c, 2, block_half(c, im, 0), a_plus)
        got(c, 1, block(c, ip))
        send(c, 3, block_half(c, ip, 1), a_minus)

    def second_axis_own(c):
        got(c, 2, block_half(c, i2, 0))
        got(c, 3, block_half(c, i2, 1))
        send(c, 4, line(c, j), b_plus)
        send(c, 5, line(c, j), b_minus)
        send(c, 6, line(c, j), sibling)

    def second_axis_forward(c):
        got(c, 4, line(c, jm))
        send(c, 7, line_half(c, jm, 0), b_plus)
        send(c, 9, line(c, jm), sibling)
        got(c, 5, line(c, jp))
        send(c, 8, line_half(c, jp, 1), b_minus)
        send(c, 10, line(c, jp), sibling)

    def second_axis_end(c):
        got(c, 7, line_half(c, j2, 0))
        send(c, 11, line_half(c, j2, 0), sibling)
        got(c, 8, line_half(c, j2, 1))
        send(c, 12, line_half(c, j2, 1), sibling)
        other = 1 - k
        got(c, 6, line(c, i, other))
        got(c, 9, line(c, im, other))
        got(c, 10, line(c, ip, other))
        got(c, 11, line_half(c, i2, 0, other))
        got(c, 12, line_half(c, i2, 1, other))

    def compute(c, g):
        total = sums.at[c % 2]

        @pl.loop(0, GROUP // UNROLL)
        def _(step):
            for u in range(UNROLL):
                t = g * GROUP + step * UNROLL + u
                col = plan[COL + t]
                x = held[c][col // 4, col % 4]
                if c == 0:
                    x = jnp.concatenate([x, jnp.ones((ONES, BLK), BF16)], axis=0)
                res = nt(x, tiles[t])
                total[t] = res[:FC]
                if c == 0:
                    degs[t] = res[FC : FC + 8]

        @pl.loop(0, GROUP // UNROLL)
        def _(step):
            for u in range(UNROLL):
                t = g * GROUP + step * UNROLL + u
                prev = plan[PREV + t]
                total[t] = total[t] + total[prev]
                if c == 0:
                    degs[t] = degs[t] + degs[prev]

    def partial(c, dest, b):
        return sums[c % 2, plan[LAST + dest * DEST + b]]

    def ring(c, s):
        for way, to in ((0, z_plus), (1, z_minus)):
            dest = (z + (NZ // 2 - s if way == 0 else NZ // 2 + s)) % NZ
            first = range(0, 2) if way == 0 else range(2, 4)
            blocks = first if s == 0 else range(DEST)
            if s > 0:
                ring_got(c, way, s - 1)
            for b in blocks:
                val = partial(c, dest, b)
                if s > 1 or (s == 1 and b in first):
                    val = val + rs_recv[c, way, s - 1, b].astype(F32)
                rs_send[c, way, s, b] = val.astype(BF16)
            here = pl.ds(blocks[0], len(blocks))
            copy = pltpu.make_async_remote_copy(
                src_ref=rs_send.at[c, way, s, here],
                dst_ref=rs_recv.at[c, way, s, here],
                send_sem=r_send.at[c, way, s],
                recv_sem=r_recv.at[c, way, s],
                device_id=to,
                device_id_type=MESH,
            )
            copy.start()
            sent.append(copy)

    def ring_got(c, way, s):
        here = pl.ds(0 if s > 0 or way == 0 else 2, 2 if s == 0 else DEST)
        pltpu.make_async_remote_copy(
            src_ref=rs_send.at[c, way, s, here],
            dst_ref=rs_recv.at[c, way, s, here],
            send_sem=r_send.at[c, way, s],
            recv_sem=r_recv.at[c, way, s],
            device_id=z_plus,
            device_id_type=MESH,
        ).wait_recv()

    def send_degrees():
        for off in range(NZ):
            dest = (z + off) % NZ
            for b in range(DEST):
                deg_send[off, b : b + 1] = degs[plan[LAST + dest * DEST + b], 0:1]
            if off:
                copy = pltpu.make_async_remote_copy(
                    src_ref=deg_send.at[off],
                    dst_ref=deg_recv.at[off],
                    send_sem=d_send.at[off],
                    recv_sem=d_recv.at[off],
                    device_id=(row, dest),
                    device_id_type=MESH,
                )
                copy.start()
                sent.append(copy)

    def sum_degrees():
        total = 1.0 + deg_send[0]
        for off in range(1, NZ):
            pltpu.make_async_remote_copy(
                src_ref=deg_send.at[off],
                dst_ref=deg_recv.at[off],
                send_sem=d_send.at[off],
                recv_sem=d_recv.at[off],
                device_id=sibling,
                device_id_type=MESH,
            ).wait_recv()
            total = total + deg_recv[off]
        deg_send[0] = total

    def finish(c):
        ring_got(c, 0, 3)
        ring_got(c, 1, 3)
        for b in range(DEST):
            val = partial(c, z, b) + rs_recv[c, 0, 3, b].astype(F32) + rs_recv[c, 1, 3, b].astype(F32)
            val = val / deg_send[0, b : b + 1]
            mean_t[c * FC : (c + 1) * FC, b * BLK : (b + 1) * BLK] = val.astype(BF16)

    for c in range(CHUNKS):
        first_axis_own(c)
    for c in range(CHUNKS):
        first_axis_forward(c)
        if c < 2:
            second_axis_own(c)
    second_axis_forward(0)
    second_axis_own(2)
    load.wait()
    for c in range(CHUNKS):
        if c + 1 < CHUNKS:
            second_axis_forward(c + 1)
        if c + 3 < CHUNKS:
            second_axis_own(c + 3)
        second_axis_end(c)
        for g in range(SLOTS // GROUP):
            if c > 0:
                ring(c - 1, g)
            compute(c, g)
        if c == 0:
            send_degrees()
        if c == 1:
            sum_degrees()
        if c > 0:
            finish(c - 1)
    for s in range(4):
        ring(CHUNKS - 1, s)
    finish(CHUNKS - 1)

    for b in range(DEST):
        here = pl.ds(b * BLK, BLK)
        total = tn(mean_t[:, here], wn_ref[...])
        total = total + jnp.dot(x_ref[here, :], ws_ref[...], preferred_element_type=F32)
        total = total + bias_ref[...]
        out_ref[here, :] = jnp.maximum(total, 0.0).astype(BF16)

    for copy in sent:
        copy.wait_send()


def per_device(
    features, adjacency, block_rows, block_cols, live_counts, self_weight, neigh_weight, out_bias
):
    rows = block_rows[0, 0]
    t = jnp.arange(SLOTS)
    live = t < live_counts[0, 0]
    same = (rows[:, None] == rows[None, :]) & live[None, :] & (t[None, :] < t[:, None])
    prev = jnp.max(jnp.where(same, t[None, :], -1), axis=1)
    here = (jnp.arange(NZ * DEST)[:, None] == rows[None, :]) & live[None, :]
    last = jnp.max(jnp.where(here, t[None, :], -1), axis=1)
    cols = jnp.clip(block_cols[0, 0], 0, 32 * DEST - 1)
    dev, part = cols // DEST, cols % DEST
    core, cx, cy = dev % 2, dev // 8, (dev // 2) % 4
    spot = jnp.where(core == 0, cy * 4 + cx, 16 + cx * 4 + cy)
    plan = jnp.concatenate(
        [spot * DEST + part, jnp.where(prev < 0, SLOTS, prev), jnp.where(last < 0, SLOTS, last)]
    ).astype(jnp.int32)

    vmem = pl.BlockSpec(memory_space=pltpu.VMEM)
    dma = pltpu.SemaphoreType.DMA
    return pl.pallas_call(
        layer_kernel,
        out_shape=jax.ShapeDtypeStruct((DEST * BLK, HID), BF16),
        in_specs=[
            pl.BlockSpec(memory_space=pltpu.SMEM),
            vmem,
            pl.BlockSpec(memory_space=pl.ANY),
            vmem,
            vmem,
            vmem,
        ],
        out_specs=vmem,
        scratch_shapes=[pltpu.VMEM((32, DEST, FC, BLK), BF16) for _ in range(CHUNKS)]
        + [
            pltpu.VMEM((SLOTS, BLK, BLK), BF16),
            pltpu.VMEM((2, SLOTS + 1, FC, BLK), F32),
            pltpu.VMEM((SLOTS + 1, 8, BLK), F32),
            pltpu.VMEM((CHUNKS, 2, 4, DEST, FC, BLK), BF16),
            pltpu.VMEM((CHUNKS, 2, 4, DEST, FC, BLK), BF16),
            pltpu.VMEM((NZ, DEST, BLK), F32),
            pltpu.VMEM((NZ, DEST, BLK), F32),
            pltpu.VMEM((FEAT, DEST * BLK), BF16),
            dma,
            dma((CHUNKS, N_GATHER)),
            dma((CHUNKS, N_GATHER)),
            dma((CHUNKS, 2, 4)),
            dma((CHUNKS, 2, 4)),
            dma((NZ,)),
            dma((NZ,)),
        ],
        compiler_params=pltpu.CompilerParams(
            collective_id=0, has_side_effects=True, vmem_limit_bytes=48 * 2**20
        ),
    )(plan, features, adjacency, self_weight, neigh_weight, out_bias.reshape(1, HID))


def solution(mesh):
    in_specs = (
        P(("row", "col"), None),
        P("row", "col", None, None, None),
        P("row", "col", None),
        P("row", "col", None),
        P("row", "col"),
        P(),
        P(),
        P(),
    )
    out_specs = P(("row", "col"), None)
    return jax.shard_map(
        per_device, mesh=mesh, in_specs=in_specs, out_specs=out_specs, check_vma=False
    )
```

```python
import functools

import jax
import jax.numpy as jnp
from jax import lax
from jax.experimental import pallas as pl
from jax.experimental.pallas import tpu as pltpu
from jax.sharding import PartitionSpec as P

MESH = pl.DeviceIdType.MESH
F32, BF16, I32 = jnp.float32, jnp.bfloat16, jnp.int32

SIDE = 4
NZ = 8
HOPS = NZ // 2
BLK = 256
FEAT = 128
HID = 256
SLOTS = 64
DEST = 4
SUB = SIDE * DEST
SIZES = (48, 32, 32, 16)
CHUNKS = len(SIZES)
STARTS = tuple(sum(SIZES[:c]) for c in range(CHUNKS))
DIRECT = (False, False, False, False)
TREE = (False, False, False, True)
PARTS = 4
ORDER = (
    ("own", 1), ("own", 0), ("ff0", 1), ("ff1", 1), ("own", 2), ("of0", 1),
    ("of1", 1), ("ff0", 0), ("ff1", 0), ("own", 3), ("of0", 0), ("ro", 1),
    ("of0", 2), ("ro", 0), ("of1", 3), ("rf1", 1), ("rf0", 1), ("ff1", 2),
    ("ff0", 2), ("of1", 0), ("of1", 2), ("ff1", 3), ("of0", 3), ("ff0", 3),
    ("rf1", 0), ("rf0", 0), ("far", 1), ("ro", 2), ("ro", 3), ("sib", 1),
    ("comp0", 1), ("comp1", 1), ("comp2", 1), ("far", 0), ("comp3", 1), ("ring0", 1),
    ("rf0", 2), ("rf1", 2), ("sib", 0), ("comp0", 0), ("comp1", 0), ("comp2", 0),
    ("comp3", 0), ("far", 2), ("ring0", 0), ("rf1", 3), ("rf0", 3), ("ring1", 1),
    ("sib", 2), ("comp0", 2), ("comp1", 2), ("comp2", 2), ("comp3", 2), ("ring0", 2),
    ("far", 3), ("ring1", 0), ("ring2", 1), ("sib", 3), ("comp0", 3), ("comp1", 3),
    ("comp2", 3), ("ring1", 2), ("comp3", 3), ("t0", 3), ("t1", 3), ("ring2", 0),
    ("ring3", 1), ("ring2", 2), ("t2", 3), ("ring3", 0), ("fin", 1), ("ring3", 2),
    ("fin", 3), ("fin", 0), ("fin", 2),
)
LEAD = 1
UNROLL = 16
ONES = 16
LANES = 128
SPOT, PREV, LAST = 0, 1, 2
N_GATHER = 16


def nt(a, b):
    return lax.dot_general(a, b, (((1,), (1,)), ((), ())), preferred_element_type=F32)


def tn(a, b):
    return lax.dot_general(a, b, (((0,), (0,)), ((), ())), preferred_element_type=F32)


def layer_kernel(
    counts,
    rows_ref,
    cols_ref,
    x_hbm,
    adj_hbm,
    ws_hbm,
    wn_hbm,
    bias_hbm,
    out_ref,
    *scratch,
):
    held, scratch = scratch[:CHUNKS], scratch[CHUNKS:]
    sums, scratch = scratch[:CHUNKS], scratch[CHUNKS:]
    rs_send, scratch = scratch[:CHUNKS], scratch[CHUNKS:]
    rs_recv, scratch = scratch[:CHUNKS], scratch[CHUNKS:]
    (
        tiles,
        degs,
        deg_send,
        deg_recv,
        degree,
        x_ref,
        ws_ref,
        wn_ref,
        bias_ref,
        acc,
        plan_v,
        plan,
        tile_sem,
        in_sem,
        g_send,
        g_recv,
        r_send,
        r_recv,
        d_send,
        d_recv,
    ) = scratch

    row, z = lax.axis_index("row"), lax.axis_index("col")
    k = row % 2
    cx, cy = row // (2 * SIDE), (row // 2) % SIDE
    i = (1 - k) * cx + k * cy
    j = (1 - k) * cy + k * cx

    def device(ii, jj):
        return (ii * (8 - 6 * k) + jj * (2 + 6 * k) + k, z)

    ip, im, i2 = (i + 1) % SIDE, (i + 3) % SIDE, (i + 2) % SIDE
    jp, jm, j2 = (j + 1) % SIDE, (j + 3) % SIDE, (j + 2) % SIDE
    a_plus, a_minus, a_far = device(ip, j), device(im, j), device(i2, j)
    b_plus, b_minus, b_far = device(i, jp), device(i, jm), device(i, j2)
    sibling = (row + 1 - 2 * k, z)
    z_plus, z_minus = (row, (z + 1) % NZ), (row, (z + NZ - 1) % NZ)
    z_plus2, z_minus2 = (row, (z + 2) % NZ), (row, (z + NZ - 2) % NZ)

    barrier = pltpu.get_barrier_semaphore()
    peers = [a_plus, a_minus, b_plus, b_minus, sibling, z_plus, z_minus]
    if any(DIRECT):
        peers += [a_far, b_far]
    if any(TREE):
        peers += [z_plus2, z_minus2]
    for peer in peers:
        pl.semaphore_signal(barrier, inc=1, device_id=peer, device_id_type=MESH)

    loads = [
        pltpu.make_async_copy(src, dst, in_sem.at[n])
        for n, (src, dst) in enumerate(
            ((x_hbm, x_ref), (ws_hbm, ws_ref), (wn_hbm, wn_ref), (bias_hbm, bias_ref))
        )
    ]
    for load in loads:
        load.start()
    tile_load = pltpu.make_async_copy(adj_hbm.at[0, 0], tiles, tile_sem)
    tile_load.start()

    loads[0].wait()
    for c in range(CHUNKS):
        eye = (
            lax.broadcasted_iota(I32, (SIZES[c], FEAT), 0) + STARTS[c]
            == lax.broadcasted_iota(I32, (SIZES[c], FEAT), 1)
        ).astype(F32).astype(BF16)
        for b in range(DEST):
            held[c][k, j, b] = nt(eye, x_ref[b * BLK : (b + 1) * BLK, :]).astype(BF16)

    pl.semaphore_wait(barrier, len(peers))

    sent = []

    def send(c, n, src, dst, to):
        copy = pltpu.make_async_remote_copy(
            src_ref=src,
            dst_ref=dst,
            send_sem=g_send.at[c, n],
            recv_sem=g_recv.at[c, n],
            device_id=to,
            device_id_type=MESH,
        )
        copy.start()
        sent.append(copy)

    def got(c, n, ref):
        pltpu.make_async_remote_copy(
            src_ref=ref,
            dst_ref=ref,
            send_sem=g_send.at[c, n],
            recv_sem=g_recv.at[c, n],
            device_id=sibling,
            device_id_type=MESH,
        ).wait_recv()

    def part(c, jj, lo, n, kk=None):
        return held[c].at[k if kk is None else kk, jj, pl.ds(lo, n)]

    def own_out(c):
        mine = part(c, j, 0, 4)
        send(c, 0, mine, part(c, j, 12, 4), a_plus)
        send(c, 1, mine, part(c, j, 4, 4), a_minus)
        if DIRECT[c]:
            send(c, 2, mine, part(c, j, 8, 4), a_far)
        send(c, 4, mine, mine, b_plus)
        send(c, 5, mine, mine, b_minus)
        if DIRECT[c]:
            send(c, 6, mine, mine, b_far)

    def first_forward(c, way):
        if way == 0:
            got(c, 0, part(c, j, 12, 4))
            if not DIRECT[c]:
                send(c, 2, part(c, j, 12, 2), part(c, j, 8, 2), a_plus)
        else:
            got(c, 1, part(c, j, 4, 4))
            if not DIRECT[c]:
                send(c, 3, part(c, j, 6, 2), part(c, j, 10, 2), a_minus)

    def own_forward(c, way):
        if way == 0:
            got(c, 4, part(c, jm, 0, 4))
            if not DIRECT[c]:
                send(c, 6, part(c, jm, 0, 2), part(c, jm, 0, 2), b_plus)
        else:
            got(c, 5, part(c, jp, 0, 4))
            if not DIRECT[c]:
                send(c, 7, part(c, jp, 2, 2), part(c, jp, 2, 2), b_minus)

    def rest_out(c):
        if DIRECT[c]:
            got(c, 2, part(c, j, 8, 4))
        else:
            got(c, 2, part(c, j, 8, 2))
            got(c, 3, part(c, j, 10, 2))
        rest = part(c, j, 4, 12)
        send(c, 8, rest, rest, b_plus)
        send(c, 9, rest, rest, b_minus)
        if DIRECT[c]:
            send(c, 10, rest, rest, b_far)
        line = part(c, j, 0, SUB)
        send(c, 12, line, line, sibling)

    def rest_forward(c, way):
        if way == 0:
            got(c, 8, part(c, jm, 4, 12))
            if not DIRECT[c]:
                send(c, 10, part(c, jm, 4, 6), part(c, jm, 4, 6), b_plus)
            line = part(c, jm, 0, SUB)
            send(c, 13, line, line, sibling)
        else:
            got(c, 9, part(c, jp, 4, 12))
            if not DIRECT[c]:
                send(c, 11, part(c, jp, 10, 6), part(c, jp, 10, 6), b_minus)
            line = part(c, jp, 0, SUB)
            send(c, 14, line, line, sibling)

    def far_in(c):
        if DIRECT[c]:
            got(c, 6, part(c, j2, 0, 4))
            got(c, 10, part(c, j2, 4, 12))
        else:
            got(c, 6, part(c, j2, 0, 2))
            got(c, 7, part(c, j2, 2, 2))
            got(c, 10, part(c, j2, 4, 6))
            got(c, 11, part(c, j2, 10, 6))
        line = part(c, j2, 0, SUB)
        send(c, 15, line, line, sibling)

    def sibling_in(c):
        for n, jj in ((12, i), (13, im), (14, ip), (15, i2)):
            got(c, n, part(c, jj, 0, SUB, 1 - k))

    def make_plan():
        t = lax.broadcasted_iota(I32, (LANES, LANES), 1)
        s = lax.broadcasted_iota(I32, (LANES, LANES), 0)
        plan_v[...] = jnp.zeros((8, LANES), I32)
        plan_v[0:1, 0:SLOTS] = rows_ref[0]
        along = jnp.broadcast_to(plan_v[0:1, :], (LANES, LANES))
        down = jnp.transpose(along)
        live = s < counts[0, 0]
        prev = jnp.max(jnp.where((along == down) & live & (s < t), s, -1), axis=0, keepdims=True)
        last = jnp.max(jnp.where((down == t) & live, s, -1), axis=0, keepdims=True)
        plan_v[0:1, 0:SLOTS] = cols_ref[0]
        cols = jnp.clip(plan_v[0:1, :], 0, 32 * DEST - 1)
        dev = cols // DEST
        ox, oy, core = dev // 8, (dev // 2) % SIDE, dev % 2
        oi = jnp.where(core == 0, ox - cx, oy - cy)
        oj = jnp.where(core == 0, oy, ox)
        plan_v[SPOT : SPOT + 1, :] = core * 64 + oj * SUB + (oi + SIDE) % SIDE * DEST + cols % DEST
        plan_v[PREV : PREV + 1, :] = jnp.where(prev < 0, SLOTS, prev)
        plan_v[LAST : LAST + 1, :] = jnp.where(last < 0, SLOTS, last)
        move = pltpu.make_async_copy(plan_v, plan, in_sem.at[4])
        move.start()
        move.wait()

    def own_part():
        for load in loads[1:]:
            load.wait()
        for b in range(DEST):
            here = pl.ds(b * BLK, BLK)
            own = jnp.dot(x_ref[here, :], ws_ref[...], preferred_element_type=F32)
            acc[here, :] = own + bias_ref[...]

    def compute(c, q):
        total, size = sums[c], SIZES[c]
        steps = SLOTS // PARTS // UNROLL

        @pl.loop(q * steps, (q + 1) * steps)
        def _(step):
            for u in range(UNROLL):
                t = step * UNROLL + u
                spot = plan[SPOT, t]
                x = held[c][spot // 64, spot // SUB % SIDE, spot % SUB]
                if c == LEAD:
                    x = jnp.concatenate([x, jnp.ones((ONES, BLK), BF16)], axis=0)
                res = nt(x, tiles[t])
                total[t] = res[:size]
                if c == LEAD:
                    degs[t] = res[size : size + 8]
            for u in range(UNROLL):
                t = step * UNROLL + u
                prev = plan[PREV, t]
                total[t] = total[t] + total[prev]
                if c == LEAD:
                    degs[t] = degs[t] + degs[prev]

    def partial(c, dest, b):
        return sums[c][plan[LAST, dest * DEST + b]]

    def degree_row(dest, b):
        return degs[plan[LAST, dest * DEST + b], 0:1]

    def ring_send(c, way, s, lo, n, to):
        here = pl.ds(lo, n)
        copy = pltpu.make_async_remote_copy(
            src_ref=rs_send[c].at[way, s, here],
            dst_ref=rs_recv[c].at[way, s, here],
            send_sem=r_send.at[c, way, s],
            recv_sem=r_recv.at[c, way, s],
            device_id=to,
            device_id_type=MESH,
        )
        copy.start()
        sent.append(copy)

    def ring(c, s):
        for way, to in ((0, z_plus), (1, z_minus)):
            dest = (z + (HOPS - s if way == 0 else HOPS + s)) % NZ
            first = range(0, 2) if way == 0 else range(2, 4)
            blocks = first if s == 0 else range(DEST)
            if s > 0:
                ring_got(c, way, s - 1, 2 if s == 1 else DEST)
            for b in blocks:
                val = partial(c, dest, b)
                if s > 1 or (s == 1 and b in first):
                    val = val + rs_recv[c][way, s - 1, b].astype(F32)
                rs_send[c][way, s, b] = val.astype(BF16)
            ring_send(c, way, s, blocks[0], len(blocks), to)
            if c == LEAD:
                degree_send(way, s, dest, blocks, (s - 1,) if s > 0 else (), to)

    def degree_send(way, s, dest, blocks, arrived, to):
        for b in range(DEST):
            val = degree_row(dest, b) if b in blocks else jnp.zeros((1, BLK), F32)
            for n in arrived:
                val = val + deg_recv[way, n, b : b + 1]
            deg_send[way, s, b : b + 1] = val
        copy = degree_copy(way, s, to)
        copy.start()
        sent.append(copy)

    def tree(c, stage):
        for way, to, to2 in ((0, z_plus, z_plus2), (1, z_minus, z_minus2)):
            sign = 1 if way == 0 else NZ - 1
            half = 2 * way
            if stage == 0:
                for b in range(DEST):
                    rs_send[c][way, 0, b] = partial(c, (z + 3 * sign) % NZ, b).astype(BF16)
                ring_send(c, way, 0, 0, DEST, to)
                if c == LEAD:
                    degree_send(way, 0, (z + 3 * sign) % NZ, range(DEST), (), to)
                for b in range(half, half + 2):
                    rs_send[c][way, 1, b] = partial(c, (z + 4) % NZ, b).astype(BF16)
                ring_send(c, way, 1, half, 2, to2)
                if c == LEAD:
                    degree_send(way, 1, (z + 4) % NZ, range(half, half + 2), (), to2)
            elif stage == 1:
                for b in range(DEST):
                    rs_send[c][way, 2, b] = partial(c, (z + sign) % NZ, b).astype(BF16)
                ring_send(c, way, 2, 0, DEST, to)
                if c == LEAD:
                    degree_send(way, 2, (z + sign) % NZ, range(DEST), (), to)
            else:
                ring_got(c, way, 0, DEST)
                ring_got(c, way, 1, 2)
                for b in range(DEST):
                    val = partial(c, (z + 2 * sign) % NZ, b) + rs_recv[c][way, 0, b].astype(F32)
                    if b in (half, half + 1):
                        val = val + rs_recv[c][way, 1, b].astype(F32)
                    rs_send[c][way, 3, b] = val.astype(BF16)
                ring_send(c, way, 3, 0, DEST, to2)
                if c == LEAD:
                    degree_send(way, 3, (z + 2 * sign) % NZ, range(DEST), (0, 1), to2)

    def degree_copy(way, s, to):
        return pltpu.make_async_remote_copy(
            src_ref=deg_send.at[way, s],
            dst_ref=deg_recv.at[way, s],
            send_sem=d_send.at[way, s],
            recv_sem=d_recv.at[way, s],
            device_id=to,
            device_id_type=MESH,
        )

    def ring_got(c, way, s, n):
        here = pl.ds(2 * way if n == 2 else 0, n)
        pltpu.make_async_remote_copy(
            src_ref=rs_send[c].at[way, s, here],
            dst_ref=rs_recv[c].at[way, s, here],
            send_sem=r_send.at[c, way, s],
            recv_sem=r_recv.at[c, way, s],
            device_id=z_plus,
            device_id_type=MESH,
        ).wait_recv()
        if c == LEAD:
            degree_copy(way, s, z_plus).wait_recv()

    def finish(c, final):
        arrived = (2, 3) if TREE[c] else (3,)
        for way in range(2):
            for s in arrived:
                ring_got(c, way, s, DEST)
        for b in range(DEST):
            if c == LEAD:
                mine = 1.0 + degree_row(z, b)
                for way in range(2):
                    for s in arrived:
                        mine = mine + deg_recv[way, s, b : b + 1]
                degree[b : b + 1] = mine
            val = partial(c, z, b)
            for way in range(2):
                for s in arrived:
                    val = val + rs_recv[c][way, s, b].astype(F32)
            mean = (val / degree[b : b + 1]).astype(BF16)
            here = pl.ds(b * BLK, BLK)
            total = acc[here, :] + tn(mean, wn_ref[STARTS[c] : STARTS[c] + SIZES[c], :])
            if final:
                out_ref[here, :] = jnp.maximum(total, 0.0).astype(BF16)
            else:
                acc[here, :] = total

    def prepare():
        for c in range(CHUNKS):
            sums[c][SLOTS] = jnp.zeros((SIZES[c], BLK), F32)
        degs[SLOTS] = jnp.zeros((8, BLK), F32)
        make_plan()
        own_part()

    run = {
        "own": own_out,
        "ff0": lambda c: first_forward(c, 0),
        "ff1": lambda c: first_forward(c, 1),
        "of0": lambda c: own_forward(c, 0),
        "of1": lambda c: own_forward(c, 1),
        "ro": rest_out,
        "rf0": lambda c: rest_forward(c, 0),
        "rf1": lambda c: rest_forward(c, 1),
        "far": far_in,
        "sib": sibling_in,
    }
    for q in range(PARTS):
        run[f"comp{q}"] = functools.partial(compute, q=q)
    for s in range(HOPS):
        run[f"ring{s}"] = functools.partial(ring, s=s)
    for stage in range(3):
        run[f"t{stage}"] = functools.partial(tree, stage=stage)
    final = [n for n, (name, _) in enumerate(ORDER) if name == "fin"][-1]
    ready = loaded = False
    for n, (name, c) in enumerate(ORDER):
        if name == "comp0" and not loaded:
            tile_load.wait()
            loaded = True
        if name != "own" and not ready:
            prepare()
            ready = True
        if name == "fin":
            finish(c, n == final)
        else:
            run[name](c)

    for copy in sent:
        copy.wait_send()


def per_device(
    features, adjacency, block_rows, block_cols, live_counts, self_weight, neigh_weight, out_bias
):
    vmem = pl.BlockSpec(memory_space=pltpu.VMEM)
    smem = pl.BlockSpec(memory_space=pltpu.SMEM)
    hbm = pl.BlockSpec(memory_space=pltpu.HBM)
    dma = pltpu.SemaphoreType.DMA
    return pl.pallas_call(
        layer_kernel,
        out_shape=jax.ShapeDtypeStruct((DEST * BLK, HID), BF16),
        in_specs=[smem, vmem, vmem, hbm, hbm, hbm, hbm, hbm],
        out_specs=vmem,
        scratch_shapes=[pltpu.VMEM((2, SIDE, SUB, size, BLK), BF16) for size in SIZES]
        + [pltpu.VMEM((SLOTS + 1, size, BLK), F32) for size in SIZES]
        + [pltpu.VMEM((2, HOPS, DEST, size, BLK), BF16) for size in SIZES]
        + [pltpu.VMEM((2, HOPS, DEST, size, BLK), BF16) for size in SIZES]
        + [
            pltpu.VMEM((SLOTS, BLK, BLK), BF16),
            pltpu.VMEM((SLOTS + 1, 8, BLK), F32),
            pltpu.VMEM((2, HOPS, DEST, BLK), F32),
            pltpu.VMEM((2, HOPS, DEST, BLK), F32),
            pltpu.VMEM((DEST, BLK), F32),
            pltpu.VMEM((DEST * BLK, FEAT), BF16),
            pltpu.VMEM((FEAT, HID), BF16),
            pltpu.VMEM((FEAT, HID), BF16),
            pltpu.VMEM((1, HID), F32),
            pltpu.VMEM((DEST * BLK, HID), F32),
            pltpu.VMEM((8, LANES), I32),
            pltpu.SMEM((8, LANES), I32),
            dma,
            dma((5,)),
            dma((CHUNKS, N_GATHER)),
            dma((CHUNKS, N_GATHER)),
            dma((CHUNKS, 2, HOPS)),
            dma((CHUNKS, 2, HOPS)),
            dma((2, HOPS)),
            dma((2, HOPS)),
        ],
        compiler_params=pltpu.CompilerParams(
            collective_id=0, has_side_effects=True, vmem_limit_bytes=56 * 2**20
        ),
    )(
        live_counts,
        block_rows,
        block_cols,
        features,
        adjacency,
        self_weight,
        neigh_weight,
        out_bias.reshape(1, HID),
    )


def solution(mesh):
    in_specs = (
        P(("row", "col"), None),
        P("row", "col", None, None, None),
        P("row", "col", None),
        P("row", "col", None),
        P("row", "col"),
        P(),
        P(),
        P(),
    )
    out_specs = P(("row", "col"), None)
    return jax.shard_map(
        per_device, mesh=mesh, in_specs=in_specs, out_specs=out_specs, check_vma=False
    )
```

```python
import functools

import jax
import jax.numpy as jnp
from jax import lax
from jax.experimental import pallas as pl
from jax.experimental.pallas import tpu as pltpu
from jax.sharding import PartitionSpec as P

MESH = pl.DeviceIdType.MESH
F32, BF16, I32 = jnp.float32, jnp.bfloat16, jnp.int32

SIDE = 4
NZ = 8
HOPS = NZ // 2
BLK = 256
FEAT = 128
HID = 256
SLOTS = 64
DEST = 4
SUB = SIDE * DEST
SIZES = (48, 48, 32)
CHUNKS = len(SIZES)
STARTS = tuple(sum(SIZES[:c]) for c in range(CHUNKS))
DIRECT = (False, False, False)
TREE = (False, False, True)
PARTS = 4
ORDER = (
    ("own", 2), ("own", 1), ("ff0", 2), ("ff1", 2), ("own", 0), ("of1", 2),
    ("of0", 2), ("ff0", 1), ("ff1", 1), ("of0", 1), ("of1", 1), ("ro", 2),
    ("ff1", 0), ("ff0", 0), ("ro", 1), ("rf0", 2), ("rf1", 2), ("ro", 0),
    ("rf0", 1), ("far", 2), ("rf1", 1), ("sib", 2), ("comp0", 2), ("of0", 0),
    ("comp1", 2), ("comp2", 2), ("of1", 0), ("rf0", 0), ("comp3", 2), ("far", 1),
    ("rf1", 0), ("t0", 2), ("t1", 2), ("sib", 1), ("comp0", 1), ("comp1", 1),
    ("comp2", 1), ("far", 0), ("comp3", 1), ("ring0", 1), ("sib", 0), ("comp0", 0),
    ("comp1", 0), ("t2", 2), ("comp2", 0), ("comp3", 0), ("ring0", 0), ("ring1", 1),
    ("fin", 2), ("ring1", 0), ("ring2", 1), ("ring2", 0), ("ring3", 1), ("ring3", 0),
    ("fin", 1), ("fin", 0),
)
LEAD = 2
UNROLL = 16
ONES = 16
LANES = 128
SPOT, PREV, LAST = 0, 1, 2
N_GATHER = 16


def nt(a, b):
    return lax.dot_general(a, b, (((1,), (1,)), ((), ())), preferred_element_type=F32)


def tn(a, b):
    return lax.dot_general(a, b, (((0,), (0,)), ((), ())), preferred_element_type=F32)


def layer_kernel(
    counts,
    rows_ref,
    cols_ref,
    x_hbm,
    adj_hbm,
    ws_hbm,
    wn_hbm,
    bias_hbm,
    out_ref,
    *scratch,
):
    held, scratch = scratch[:CHUNKS], scratch[CHUNKS:]
    sums, scratch = scratch[:CHUNKS], scratch[CHUNKS:]
    rs_send, scratch = scratch[:CHUNKS], scratch[CHUNKS:]
    rs_recv, scratch = scratch[:CHUNKS], scratch[CHUNKS:]
    (
        tiles,
        degs,
        deg_send,
        deg_recv,
        degree,
        x_ref,
        ws_ref,
        wn_ref,
        bias_ref,
        acc,
        plan_v,
        plan,
        tile_sem,
        in_sem,
        g_send,
        g_recv,
        r_send,
        r_recv,
        d_send,
        d_recv,
    ) = scratch

    row, z = lax.axis_index("row"), lax.axis_index("col")
    k = row % 2
    cx, cy = row // (2 * SIDE), (row // 2) % SIDE
    i = (1 - k) * cx + k * cy
    j = (1 - k) * cy + k * cx

    def device(ii, jj):
        return (ii * (8 - 6 * k) + jj * (2 + 6 * k) + k, z)

    ip, im, i2 = (i + 1) % SIDE, (i + 3) % SIDE, (i + 2) % SIDE
    jp, jm, j2 = (j + 1) % SIDE, (j + 3) % SIDE, (j + 2) % SIDE
    a_plus, a_minus, a_far = device(ip, j), device(im, j), device(i2, j)
    b_plus, b_minus, b_far = device(i, jp), device(i, jm), device(i, j2)
    sibling = (row + 1 - 2 * k, z)
    z_plus, z_minus = (row, (z + 1) % NZ), (row, (z + NZ - 1) % NZ)
    z_plus2, z_minus2 = (row, (z + 2) % NZ), (row, (z + NZ - 2) % NZ)

    barrier = pltpu.get_barrier_semaphore()
    peers = [a_plus, a_minus, b_plus, b_minus, sibling, z_plus, z_minus]
    if any(DIRECT):
        peers += [a_far, b_far]
    if any(TREE):
        peers += [z_plus2, z_minus2]
    for peer in peers:
        pl.semaphore_signal(barrier, inc=1, device_id=peer, device_id_type=MESH)

    loads = [
        pltpu.make_async_copy(src, dst, in_sem.at[n])
        for n, (src, dst) in enumerate(
            ((x_hbm, x_ref), (ws_hbm, ws_ref), (wn_hbm, wn_ref), (bias_hbm, bias_ref))
        )
    ]
    for load in loads:
        load.start()
    tile_load = pltpu.make_async_copy(adj_hbm.at[0, 0], tiles, tile_sem)
    tile_load.start()

    loads[0].wait()
    for c in range(CHUNKS):
        eye = (
            lax.broadcasted_iota(I32, (SIZES[c], FEAT), 0) + STARTS[c]
            == lax.broadcasted_iota(I32, (SIZES[c], FEAT), 1)
        ).astype(F32).astype(BF16)
        for b in range(DEST):
            held[c][k, j, b] = nt(eye, x_ref[b * BLK : (b + 1) * BLK, :]).astype(BF16)

    pl.semaphore_wait(barrier, len(peers))

    sent = []

    def send(c, n, src, dst, to):
        copy = pltpu.make_async_remote_copy(
            src_ref=src,
            dst_ref=dst,
            send_sem=g_send.at[c, n],
            recv_sem=g_recv.at[c, n],
            device_id=to,
            device_id_type=MESH,
        )
        copy.start()
        sent.append(copy)

    def got(c, n, ref):
        pltpu.make_async_remote_copy(
            src_ref=ref,
            dst_ref=ref,
            send_sem=g_send.at[c, n],
            recv_sem=g_recv.at[c, n],
            device_id=sibling,
            device_id_type=MESH,
        ).wait_recv()

    def part(c, jj, lo, n, kk=None):
        return held[c].at[k if kk is None else kk, jj, pl.ds(lo, n)]

    def own_out(c):
        mine = part(c, j, 0, 4)
        send(c, 0, mine, part(c, j, 12, 4), a_plus)
        send(c, 1, mine, part(c, j, 4, 4), a_minus)
        if DIRECT[c]:
            send(c, 2, mine, part(c, j, 8, 4), a_far)
        send(c, 4, mine, mine, b_plus)
        send(c, 5, mine, mine, b_minus)
        if DIRECT[c]:
            send(c, 6, mine, mine, b_far)

    def first_forward(c, way):
        if way == 0:
            got(c, 0, part(c, j, 12, 4))
            if not DIRECT[c]:
                send(c, 2, part(c, j, 12, 2), part(c, j, 8, 2), a_plus)
        else:
            got(c, 1, part(c, j, 4, 4))
            if not DIRECT[c]:
                send(c, 3, part(c, j, 6, 2), part(c, j, 10, 2), a_minus)

    def own_forward(c, way):
        if way == 0:
            got(c, 4, part(c, jm, 0, 4))
            if not DIRECT[c]:
                send(c, 6, part(c, jm, 0, 2), part(c, jm, 0, 2), b_plus)
        else:
            got(c, 5, part(c, jp, 0, 4))
            if not DIRECT[c]:
                send(c, 7, part(c, jp, 2, 2), part(c, jp, 2, 2), b_minus)

    def rest_out(c):
        if DIRECT[c]:
            got(c, 2, part(c, j, 8, 4))
        else:
            got(c, 2, part(c, j, 8, 2))
            got(c, 3, part(c, j, 10, 2))
        rest = part(c, j, 4, 12)
        send(c, 8, rest, rest, b_plus)
        send(c, 9, rest, rest, b_minus)
        if DIRECT[c]:
            send(c, 10, rest, rest, b_far)
        line = part(c, j, 0, SUB)
        send(c, 12, line, line, sibling)

    def rest_forward(c, way):
        if way == 0:
            got(c, 8, part(c, jm, 4, 12))
            if not DIRECT[c]:
                send(c, 10, part(c, jm, 4, 6), part(c, jm, 4, 6), b_plus)
            line = part(c, jm, 0, SUB)
            send(c, 13, line, line, sibling)
        else:
            got(c, 9, part(c, jp, 4, 12))
            if not DIRECT[c]:
                send(c, 11, part(c, jp, 10, 6), part(c, jp, 10, 6), b_minus)
            line = part(c, jp, 0, SUB)
            send(c, 14, line, line, sibling)

    def far_in(c):
        if DIRECT[c]:
            got(c, 6, part(c, j2, 0, 4))
            got(c, 10, part(c, j2, 4, 12))
        else:
            got(c, 6, part(c, j2, 0, 2))
            got(c, 7, part(c, j2, 2, 2))
            got(c, 10, part(c, j2, 4, 6))
            got(c, 11, part(c, j2, 10, 6))
        line = part(c, j2, 0, SUB)
        send(c, 15, line, line, sibling)

    def sibling_in(c):
        for n, jj in ((12, i), (13, im), (14, ip), (15, i2)):
            got(c, n, part(c, jj, 0, SUB, 1 - k))

    def make_plan():
        t = lax.broadcasted_iota(I32, (LANES, LANES), 1)
        s = lax.broadcasted_iota(I32, (LANES, LANES), 0)
        plan_v[...] = jnp.zeros((8, LANES), I32)
        plan_v[0:1, 0:SLOTS] = rows_ref[0]
        along = jnp.broadcast_to(plan_v[0:1, :], (LANES, LANES))
        down = jnp.transpose(along)
        live = s < counts[0, 0]
        prev = jnp.max(jnp.where((along == down) & live & (s < t), s, -1), axis=0, keepdims=True)
        last = jnp.max(jnp.where((down == t) & live, s, -1), axis=0, keepdims=True)
        plan_v[0:1, 0:SLOTS] = cols_ref[0]
        cols = jnp.clip(plan_v[0:1, :], 0, 32 * DEST - 1)
        dev = cols // DEST
        ox, oy, core = dev // 8, (dev // 2) % SIDE, dev % 2
        oi = jnp.where(core == 0, ox - cx, oy - cy)
        oj = jnp.where(core == 0, oy, ox)
        plan_v[SPOT : SPOT + 1, :] = core * 64 + oj * SUB + (oi + SIDE) % SIDE * DEST + cols % DEST
        plan_v[PREV : PREV + 1, :] = jnp.where(prev < 0, SLOTS, prev)
        plan_v[LAST : LAST + 1, :] = jnp.where(last < 0, SLOTS, last)
        move = pltpu.make_async_copy(plan_v, plan, in_sem.at[4])
        move.start()
        move.wait()

    def own_part():
        for load in loads[1:]:
            load.wait()
        for b in range(DEST):
            here = pl.ds(b * BLK, BLK)
            own = jnp.dot(x_ref[here, :], ws_ref[...], preferred_element_type=F32)
            acc[here, :] = own + bias_ref[...]

    def compute(c, q):
        total, size = sums[c], SIZES[c]
        steps = SLOTS // PARTS // UNROLL

        @pl.loop(q * steps, (q + 1) * steps)
        def _(step):
            for u in range(UNROLL):
                t = step * UNROLL + u
                spot = plan[SPOT, t]
                x = held[c][spot // 64, spot // SUB % SIDE, spot % SUB]
                if c == LEAD:
                    x = jnp.concatenate([x, jnp.ones((ONES, BLK), BF16)], axis=0)
                res = nt(x, tiles[t])
                total[t] = res[:size]
                if c == LEAD:
                    degs[t] = res[size : size + 8]
            for u in range(UNROLL):
                t = step * UNROLL + u
                prev = plan[PREV, t]
                total[t] = total[t] + total[prev]
                if c == LEAD:
                    degs[t] = degs[t] + degs[prev]

    def partial(c, dest, b):
        return sums[c][plan[LAST, dest * DEST + b]]

    def degree_row(dest, b):
        return degs[plan[LAST, dest * DEST + b], 0:1]

    def ring_send(c, way, s, lo, n, to):
        here = pl.ds(lo, n)
        copy = pltpu.make_async_remote_copy(
            src_ref=rs_send[c].at[way, s, here],
            dst_ref=rs_recv[c].at[way, s, here],
            send_sem=r_send.at[c, way, s],
            recv_sem=r_recv.at[c, way, s],
            device_id=to,
            device_id_type=MESH,
        )
        copy.start()
        sent.append(copy)

    def ring(c, s):
        for way, to in ((0, z_plus), (1, z_minus)):
            dest = (z + (HOPS - s if way == 0 else HOPS + s)) % NZ
            first = range(0, 2) if way == 0 else range(2, 4)
            blocks = first if s == 0 else range(DEST)
            if s > 0:
                ring_got(c, way, s - 1, 2 if s == 1 else DEST)
            for b in blocks:
                val = partial(c, dest, b)
                if s > 1 or (s == 1 and b in first):
                    val = val + rs_recv[c][way, s - 1, b].astype(F32)
                rs_send[c][way, s, b] = val.astype(BF16)
            ring_send(c, way, s, blocks[0], len(blocks), to)
            if c == LEAD:
                degree_send(way, s, dest, blocks, (s - 1,) if s > 0 else (), to)

    def degree_send(way, s, dest, blocks, arrived, to):
        for b in range(DEST):
            val = degree_row(dest, b) if b in blocks else jnp.zeros((1, BLK), F32)
            for n in arrived:
                val = val + deg_recv[way, n, b : b + 1]
            deg_send[way, s, b : b + 1] = val
        copy = degree_copy(way, s, to)
        copy.start()
        sent.append(copy)

    def tree(c, stage):
        for way, to, to2 in ((0, z_plus, z_plus2), (1, z_minus, z_minus2)):
            sign = 1 if way == 0 else NZ - 1
            half = 2 * way
            if stage == 0:
                for b in range(DEST):
                    rs_send[c][way, 0, b] = partial(c, (z + 3 * sign) % NZ, b).astype(BF16)
                ring_send(c, way, 0, 0, DEST, to)
                if c == LEAD:
                    degree_send(way, 0, (z + 3 * sign) % NZ, range(DEST), (), to)
                for b in range(half, half + 2):
                    rs_send[c][way, 1, b] = partial(c, (z + 4) % NZ, b).astype(BF16)
                ring_send(c, way, 1, half, 2, to2)
                if c == LEAD:
                    degree_send(way, 1, (z + 4) % NZ, range(half, half + 2), (), to2)
            elif stage == 1:
                for b in range(DEST):
                    rs_send[c][way, 2, b] = partial(c, (z + sign) % NZ, b).astype(BF16)
                ring_send(c, way, 2, 0, DEST, to)
                if c == LEAD:
                    degree_send(way, 2, (z + sign) % NZ, range(DEST), (), to)
            else:
                ring_got(c, way, 0, DEST)
                ring_got(c, way, 1, 2)
                for b in range(DEST):
                    val = partial(c, (z + 2 * sign) % NZ, b) + rs_recv[c][way, 0, b].astype(F32)
                    if b in (half, half + 1):
                        val = val + rs_recv[c][way, 1, b].astype(F32)
                    rs_send[c][way, 3, b] = val.astype(BF16)
                ring_send(c, way, 3, 0, DEST, to2)
                if c == LEAD:
                    degree_send(way, 3, (z + 2 * sign) % NZ, range(DEST), (0, 1), to2)

    def degree_copy(way, s, to):
        return pltpu.make_async_remote_copy(
            src_ref=deg_send.at[way, s],
            dst_ref=deg_recv.at[way, s],
            send_sem=d_send.at[way, s],
            recv_sem=d_recv.at[way, s],
            device_id=to,
            device_id_type=MESH,
        )

    def ring_got(c, way, s, n):
        here = pl.ds(2 * way if n == 2 else 0, n)
        pltpu.make_async_remote_copy(
            src_ref=rs_send[c].at[way, s, here],
            dst_ref=rs_recv[c].at[way, s, here],
            send_sem=r_send.at[c, way, s],
            recv_sem=r_recv.at[c, way, s],
            device_id=z_plus,
            device_id_type=MESH,
        ).wait_recv()
        if c == LEAD:
            degree_copy(way, s, z_plus).wait_recv()

    def finish(c, final):
        arrived = (2, 3) if TREE[c] else (3,)
        for way in range(2):
            for s in arrived:
                ring_got(c, way, s, DEST)
        for b in range(DEST):
            if c == LEAD:
                mine = 1.0 + degree_row(z, b)
                for way in range(2):
                    for s in arrived:
                        mine = mine + deg_recv[way, s, b : b + 1]
                degree[b : b + 1] = mine
            val = partial(c, z, b)
            for way in range(2):
                for s in arrived:
                    val = val + rs_recv[c][way, s, b].astype(F32)
            mean = (val / degree[b : b + 1]).astype(BF16)
            here = pl.ds(b * BLK, BLK)
            total = acc[here, :] + tn(mean, wn_ref[STARTS[c] : STARTS[c] + SIZES[c], :])
            if final:
                out_ref[here, :] = jnp.maximum(total, 0.0).astype(BF16)
            else:
                acc[here, :] = total

    def prepare():
        for c in range(CHUNKS):
            sums[c][SLOTS] = jnp.zeros((SIZES[c], BLK), F32)
        degs[SLOTS] = jnp.zeros((8, BLK), F32)
        make_plan()
        own_part()

    run = {
        "own": own_out,
        "ff0": lambda c: first_forward(c, 0),
        "ff1": lambda c: first_forward(c, 1),
        "of0": lambda c: own_forward(c, 0),
        "of1": lambda c: own_forward(c, 1),
        "ro": rest_out,
        "rf0": lambda c: rest_forward(c, 0),
        "rf1": lambda c: rest_forward(c, 1),
        "far": far_in,
        "sib": sibling_in,
    }
    for q in range(PARTS):
        run[f"comp{q}"] = functools.partial(compute, q=q)
    for s in range(HOPS):
        run[f"ring{s}"] = functools.partial(ring, s=s)
    for stage in range(3):
        run[f"t{stage}"] = functools.partial(tree, stage=stage)
    final = [n for n, (name, _) in enumerate(ORDER) if name == "fin"][-1]
    ready = loaded = False
    for n, (name, c) in enumerate(ORDER):
        if name == "comp0" and not loaded:
            tile_load.wait()
            loaded = True
        if name != "own" and not ready:
            prepare()
            ready = True
        if name == "fin":
            finish(c, n == final)
        else:
            run[name](c)

    for copy in sent:
        copy.wait_send()


def per_device(
    features, adjacency, block_rows, block_cols, live_counts, self_weight, neigh_weight, out_bias
):
    vmem = pl.BlockSpec(memory_space=pltpu.VMEM)
    smem = pl.BlockSpec(memory_space=pltpu.SMEM)
    hbm = pl.BlockSpec(memory_space=pltpu.HBM)
    dma = pltpu.SemaphoreType.DMA
    return pl.pallas_call(
        layer_kernel,
        out_shape=pltpu.VMEM((DEST * BLK, HID), BF16),
        in_specs=[smem, vmem, vmem, hbm, hbm, hbm, hbm, hbm],
        out_specs=vmem,
        scratch_shapes=[pltpu.VMEM((2, SIDE, SUB, size, BLK), BF16) for size in SIZES]
        + [pltpu.VMEM((SLOTS + 1, size, BLK), F32) for size in SIZES]
        + [pltpu.VMEM((2, HOPS, DEST, size, BLK), BF16) for size in SIZES]
        + [pltpu.VMEM((2, HOPS, DEST, size, BLK), BF16) for size in SIZES]
        + [
            pltpu.VMEM((SLOTS, BLK, BLK), BF16),
            pltpu.VMEM((SLOTS + 1, 8, BLK), F32),
            pltpu.VMEM((2, HOPS, DEST, BLK), F32),
            pltpu.VMEM((2, HOPS, DEST, BLK), F32),
            pltpu.VMEM((DEST, BLK), F32),
            pltpu.VMEM((DEST * BLK, FEAT), BF16),
            pltpu.VMEM((FEAT, HID), BF16),
            pltpu.VMEM((FEAT, HID), BF16),
            pltpu.VMEM((1, HID), F32),
            pltpu.VMEM((DEST * BLK, HID), F32),
            pltpu.VMEM((8, LANES), I32),
            pltpu.SMEM((8, LANES), I32),
            dma,
            dma((5,)),
            dma((CHUNKS, N_GATHER)),
            dma((CHUNKS, N_GATHER)),
            dma((CHUNKS, 2, HOPS)),
            dma((CHUNKS, 2, HOPS)),
            dma((2, HOPS)),
            dma((2, HOPS)),
        ],
        compiler_params=pltpu.CompilerParams(
            collective_id=0, has_side_effects=True, vmem_limit_bytes=56 * 2**20
        ),
    )(
        live_counts,
        block_rows,
        block_cols,
        features,
        adjacency,
        self_weight,
        neigh_weight,
        out_bias.reshape(1, HID),
    )


def solution(mesh):
    in_specs = (
        P(("row", "col"), None),
        P("row", "col", None, None, None),
        P("row", "col", None),
        P("row", "col", None),
        P("row", "col"),
        P(),
        P(),
        P(),
    )
    out_specs = P(("row", "col"), None)
    return jax.shard_map(
        per_device, mesh=mesh, in_specs=in_specs, out_specs=out_specs, check_vma=False
    )
```

```python
import functools

import jax
import jax.numpy as jnp
from jax import lax
from jax.experimental import pallas as pl
from jax.experimental.pallas import tpu as pltpu
from jax.sharding import PartitionSpec as P

MESH = pl.DeviceIdType.MESH
F32, BF16, I32 = jnp.float32, jnp.bfloat16, jnp.int32

SIDE = 4
NZ = 8
HOPS = NZ // 2
BLK = 256
FEAT = 128
HID = 256
SLOTS = 64
DEST = 4
SUB = SIDE * DEST
SIZES = (48, 48, 32)
CHUNKS = len(SIZES)
STARTS = tuple(sum(SIZES[:c]) for c in range(CHUNKS))
DIRECT = (False, False, False)
TREE = (False, False, True)
PARTS = 4
ORDER = (
    ("own", 2), ("own", 1), ("ff0", 2), ("ff1", 2), ("own", 0), ("of1", 2),
    ("of0", 2), ("ff0", 1), ("ff1", 1), ("of0", 1), ("of1", 1), ("ro", 2),
    ("ff1", 0), ("ff0", 0), ("ro", 1), ("rf0", 2), ("rf1", 2), ("ro", 0),
    ("rf0", 1), ("far", 2), ("rf1", 1), ("sib", 2), ("comp0", 2), ("of0", 0),
    ("comp1", 2), ("comp2", 2), ("of1", 0), ("rf0", 0), ("comp3", 2), ("far", 1),
    ("rf1", 0), ("t0", 2), ("t1", 2), ("sib", 1), ("comp0", 1), ("comp1", 1),
    ("comp2", 1), ("far", 0), ("comp3", 1), ("ring0", 1), ("sib", 0), ("comp0", 0),
    ("comp1", 0), ("t2", 2), ("comp2", 0), ("comp3", 0), ("ring0", 0), ("ring1", 1),
    ("fin", 2), ("ring1", 0), ("ring2", 1), ("ring2", 0), ("ring3", 1), ("ring3", 0),
    ("fin", 1), ("fin", 0),
)
LEAD = 2
UNROLL = 16
ONES = 16
LANES = 128
SPOT, PREV, LAST = 0, 1, 2
N_GATHER = 16


def nt(a, b):
    return lax.dot_general(a, b, (((1,), (1,)), ((), ())), preferred_element_type=F32)


def tn(a, b):
    return lax.dot_general(a, b, (((0,), (0,)), ((), ())), preferred_element_type=F32)


def layer_kernel(
    counts,
    rows_ref,
    cols_ref,
    x_hbm,
    adj_hbm,
    ws_hbm,
    wn_hbm,
    bias_hbm,
    out_ref,
    *scratch,
):
    held, scratch = scratch[:CHUNKS], scratch[CHUNKS:]
    sums, scratch = scratch[:CHUNKS], scratch[CHUNKS:]
    rs_send, scratch = scratch[:CHUNKS], scratch[CHUNKS:]
    rs_recv, scratch = scratch[:CHUNKS], scratch[CHUNKS:]
    (
        tiles,
        degs,
        deg_send,
        deg_recv,
        degree,
        x_ref,
        ws_ref,
        wn_ref,
        bias_ref,
        acc,
        plan_v,
        plan,
        tile_sem,
        in_sem,
        g_send,
        g_recv,
        r_send,
        r_recv,
        d_send,
        d_recv,
    ) = scratch

    row, z = lax.axis_index("row"), lax.axis_index("col")
    k = row % 2
    cx, cy = row // (2 * SIDE), (row // 2) % SIDE
    i = (1 - k) * cx + k * cy
    j = (1 - k) * cy + k * cx

    def device(ii, jj):
        return (ii * (8 - 6 * k) + jj * (2 + 6 * k) + k, z)

    ip, im, i2 = (i + 1) % SIDE, (i + 3) % SIDE, (i + 2) % SIDE
    jp, jm, j2 = (j + 1) % SIDE, (j + 3) % SIDE, (j + 2) % SIDE
    a_plus, a_minus, a_far = device(ip, j), device(im, j), device(i2, j)
    b_plus, b_minus, b_far = device(i, jp), device(i, jm), device(i, j2)
    sibling = (row + 1 - 2 * k, z)
    z_plus, z_minus = (row, (z + 1) % NZ), (row, (z + NZ - 1) % NZ)
    z_plus2, z_minus2 = (row, (z + 2) % NZ), (row, (z + NZ - 2) % NZ)

    barrier = pltpu.get_barrier_semaphore()
    peers = [a_plus, a_minus, b_plus, b_minus, sibling, z_plus, z_minus]
    if any(DIRECT):
        peers += [a_far, b_far]
    if any(TREE):
        peers += [z_plus2, z_minus2]
    for peer in peers:
        pl.semaphore_signal(barrier, inc=1, device_id=peer, device_id_type=MESH)

    loads = [
        pltpu.make_async_copy(src, dst, in_sem.at[n])
        for n, (src, dst) in enumerate(
            ((x_hbm, x_ref), (ws_hbm, ws_ref), (wn_hbm, wn_ref), (bias_hbm, bias_ref))
        )
    ]
    for load in loads:
        load.start()
    tile_load = pltpu.make_async_copy(adj_hbm.at[0, 0], tiles, tile_sem)
    tile_load.start()

    def transpose(c):
        eye = (
            lax.broadcasted_iota(I32, (SIZES[c], FEAT), 0) + STARTS[c]
            == lax.broadcasted_iota(I32, (SIZES[c], FEAT), 1)
        ).astype(F32).astype(BF16)
        for b in range(DEST):
            held[c][k, j, b] = nt(eye, x_ref[b * BLK : (b + 1) * BLK, :]).astype(BF16)

    loads[0].wait()
    started = ORDER[0][1]
    transpose(started)
    for c in range(CHUNKS):
        sums[c][SLOTS] = jnp.zeros((SIZES[c], BLK), F32)
    degs[SLOTS] = jnp.zeros((8, BLK), F32)
    pl.semaphore_wait(barrier, len(peers))

    sent = []

    def send(c, n, src, dst, to):
        copy = pltpu.make_async_remote_copy(
            src_ref=src,
            dst_ref=dst,
            send_sem=g_send.at[c, n],
            recv_sem=g_recv.at[c, n],
            device_id=to,
            device_id_type=MESH,
        )
        copy.start()
        sent.append(copy)

    def got(c, n, ref):
        pltpu.make_async_remote_copy(
            src_ref=ref,
            dst_ref=ref,
            send_sem=g_send.at[c, n],
            recv_sem=g_recv.at[c, n],
            device_id=sibling,
            device_id_type=MESH,
        ).wait_recv()

    def part(c, jj, lo, n, kk=None):
        return held[c].at[k if kk is None else kk, jj, pl.ds(lo, n)]

    def own_out(c):
        if c != started:
            transpose(c)
        mine = part(c, j, 0, 4)
        send(c, 0, mine, part(c, j, 12, 4), a_plus)
        send(c, 1, mine, part(c, j, 4, 4), a_minus)
        if DIRECT[c]:
            send(c, 2, mine, part(c, j, 8, 4), a_far)
        send(c, 4, mine, mine, b_plus)
        send(c, 5, mine, mine, b_minus)
        if DIRECT[c]:
            send(c, 6, mine, mine, b_far)

    def first_forward(c, way):
        if way == 0:
            got(c, 0, part(c, j, 12, 4))
            if not DIRECT[c]:
                send(c, 2, part(c, j, 12, 2), part(c, j, 8, 2), a_plus)
        else:
            got(c, 1, part(c, j, 4, 4))
            if not DIRECT[c]:
                send(c, 3, part(c, j, 6, 2), part(c, j, 10, 2), a_minus)

    def own_forward(c, way):
        if way == 0:
            got(c, 4, part(c, jm, 0, 4))
            if not DIRECT[c]:
                send(c, 6, part(c, jm, 0, 2), part(c, jm, 0, 2), b_plus)
        else:
            got(c, 5, part(c, jp, 0, 4))
            if not DIRECT[c]:
                send(c, 7, part(c, jp, 2, 2), part(c, jp, 2, 2), b_minus)

    def rest_out(c):
        if DIRECT[c]:
            got(c, 2, part(c, j, 8, 4))
        else:
            got(c, 2, part(c, j, 8, 2))
            got(c, 3, part(c, j, 10, 2))
        rest = part(c, j, 4, 12)
        send(c, 8, rest, rest, b_plus)
        send(c, 9, rest, rest, b_minus)
        if DIRECT[c]:
            send(c, 10, rest, rest, b_far)
        line = part(c, j, 0, SUB)
        send(c, 12, line, line, sibling)

    def rest_forward(c, way):
        if way == 0:
            got(c, 8, part(c, jm, 4, 12))
            if not DIRECT[c]:
                send(c, 10, part(c, jm, 4, 6), part(c, jm, 4, 6), b_plus)
            line = part(c, jm, 0, SUB)
            send(c, 13, line, line, sibling)
        else:
            got(c, 9, part(c, jp, 4, 12))
            if not DIRECT[c]:
                send(c, 11, part(c, jp, 10, 6), part(c, jp, 10, 6), b_minus)
            line = part(c, jp, 0, SUB)
            send(c, 14, line, line, sibling)

    def far_in(c):
        if DIRECT[c]:
            got(c, 6, part(c, j2, 0, 4))
            got(c, 10, part(c, j2, 4, 12))
        else:
            got(c, 6, part(c, j2, 0, 2))
            got(c, 7, part(c, j2, 2, 2))
            got(c, 10, part(c, j2, 4, 6))
            got(c, 11, part(c, j2, 10, 6))
        line = part(c, j2, 0, SUB)
        send(c, 15, line, line, sibling)

    def sibling_in(c):
        for n, jj in ((12, i), (13, im), (14, ip), (15, i2)):
            got(c, n, part(c, jj, 0, SUB, 1 - k))

    def make_plan():
        t = lax.broadcasted_iota(I32, (LANES, LANES), 1)
        s = lax.broadcasted_iota(I32, (LANES, LANES), 0)
        plan_v[...] = jnp.zeros((8, LANES), I32)
        plan_v[0:1, 0:SLOTS] = rows_ref[0]
        along = jnp.broadcast_to(plan_v[0:1, :], (LANES, LANES))
        down = jnp.transpose(along)
        live = s < counts[0, 0]
        prev = jnp.max(jnp.where((along == down) & live & (s < t), s, -1), axis=0, keepdims=True)
        last = jnp.max(jnp.where((down == t) & live, s, -1), axis=0, keepdims=True)
        plan_v[0:1, 0:SLOTS] = cols_ref[0]
        cols = jnp.clip(plan_v[0:1, :], 0, 32 * DEST - 1)
        dev = cols // DEST
        ox, oy, core = dev // 8, (dev // 2) % SIDE, dev % 2
        oi = jnp.where(core == 0, ox - cx, oy - cy)
        oj = jnp.where(core == 0, oy, ox)
        plan_v[SPOT : SPOT + 1, :] = core * 64 + oj * SUB + (oi + SIDE) % SIDE * DEST + cols % DEST
        plan_v[PREV : PREV + 1, :] = jnp.where(prev < 0, SLOTS, prev)
        plan_v[LAST : LAST + 1, :] = jnp.where(last < 0, SLOTS, last)
        move = pltpu.make_async_copy(plan_v, plan, in_sem.at[4])
        move.start()
        move.wait()

    def own_part():
        for load in loads[1:]:
            load.wait()
        for b in range(DEST):
            here = pl.ds(b * BLK, BLK)
            own = jnp.dot(x_ref[here, :], ws_ref[...], preferred_element_type=F32)
            acc[here, :] = own + bias_ref[...]

    def compute(c, q):
        total, size = sums[c], SIZES[c]
        steps = SLOTS // PARTS // UNROLL

        @pl.loop(q * steps, (q + 1) * steps)
        def _(step):
            for u in range(UNROLL):
                t = step * UNROLL + u
                spot = plan[SPOT, t]
                x = held[c][spot // 64, spot // SUB % SIDE, spot % SUB]
                if c == LEAD:
                    x = jnp.concatenate([x, jnp.ones((ONES, BLK), BF16)], axis=0)
                res = nt(x, tiles[t])
                total[t] = res[:size]
                if c == LEAD:
                    degs[t] = res[size : size + 8]
            for u in range(UNROLL):
                t = step * UNROLL + u
                prev = plan[PREV, t]
                total[t] = total[t] + total[prev]
                if c == LEAD:
                    degs[t] = degs[t] + degs[prev]

    def partial(c, dest, b):
        return sums[c][plan[LAST, dest * DEST + b]]

    def degree_row(dest, b):
        return degs[plan[LAST, dest * DEST + b], 0:1]

    def ring_send(c, way, s, lo, n, to):
        here = pl.ds(lo, n)
        copy = pltpu.make_async_remote_copy(
            src_ref=rs_send[c].at[way, s, here],
            dst_ref=rs_recv[c].at[way, s, here],
            send_sem=r_send.at[c, way, s],
            recv_sem=r_recv.at[c, way, s],
            device_id=to,
            device_id_type=MESH,
        )
        copy.start()
        sent.append(copy)

    def ring(c, s):
        for way, to in ((0, z_plus), (1, z_minus)):
            dest = (z + (HOPS - s if way == 0 else HOPS + s)) % NZ
            first = range(0, 2) if way == 0 else range(2, 4)
            blocks = first if s == 0 else range(DEST)
            if s > 0:
                ring_got(c, way, s - 1, 2 if s == 1 else DEST)
            for b in blocks:
                val = partial(c, dest, b)
                if s > 1 or (s == 1 and b in first):
                    val = val + rs_recv[c][way, s - 1, b].astype(F32)
                rs_send[c][way, s, b] = val.astype(BF16)
            ring_send(c, way, s, blocks[0], len(blocks), to)
            if c == LEAD:
                degree_send(way, s, dest, blocks, (s - 1,) if s > 0 else (), to)

    def degree_send(way, s, dest, blocks, arrived, to):
        for b in range(DEST):
            val = degree_row(dest, b) if b in blocks else jnp.zeros((1, BLK), F32)
            for n in arrived:
                val = val + deg_recv[way, n, b : b + 1]
            deg_send[way, s, b : b + 1] = val
        copy = degree_copy(way, s, to)
        copy.start()
        sent.append(copy)

    def tree(c, stage):
        for way, to, to2 in ((0, z_plus, z_plus2), (1, z_minus, z_minus2)):
            sign = 1 if way == 0 else NZ - 1
            half = 2 * way
            if stage == 0:
                for b in range(DEST):
                    rs_send[c][way, 0, b] = partial(c, (z + 3 * sign) % NZ, b).astype(BF16)
                ring_send(c, way, 0, 0, DEST, to)
                if c == LEAD:
                    degree_send(way, 0, (z + 3 * sign) % NZ, range(DEST), (), to)
                for b in range(half, half + 2):
                    rs_send[c][way, 1, b] = partial(c, (z + 4) % NZ, b).astype(BF16)
                ring_send(c, way, 1, half, 2, to2)
                if c == LEAD:
                    degree_send(way, 1, (z + 4) % NZ, range(half, half + 2), (), to2)
            elif stage == 1:
                for b in range(DEST):
                    rs_send[c][way, 2, b] = partial(c, (z + sign) % NZ, b).astype(BF16)
                ring_send(c, way, 2, 0, DEST, to)
                if c == LEAD:
                    degree_send(way, 2, (z + sign) % NZ, range(DEST), (), to)
            else:
                ring_got(c, way, 0, DEST)
                ring_got(c, way, 1, 2)
                for b in range(DEST):
                    val = partial(c, (z + 2 * sign) % NZ, b) + rs_recv[c][way, 0, b].astype(F32)
                    if b in (half, half + 1):
                        val = val + rs_recv[c][way, 1, b].astype(F32)
                    rs_send[c][way, 3, b] = val.astype(BF16)
                ring_send(c, way, 3, 0, DEST, to2)
                if c == LEAD:
                    degree_send(way, 3, (z + 2 * sign) % NZ, range(DEST), (0, 1), to2)

    def degree_copy(way, s, to):
        return pltpu.make_async_remote_copy(
            src_ref=deg_send.at[way, s],
            dst_ref=deg_recv.at[way, s],
            send_sem=d_send.at[way, s],
            recv_sem=d_recv.at[way, s],
            device_id=to,
            device_id_type=MESH,
        )

    def ring_got(c, way, s, n):
        here = pl.ds(2 * way if n == 2 else 0, n)
        pltpu.make_async_remote_copy(
            src_ref=rs_send[c].at[way, s, here],
            dst_ref=rs_recv[c].at[way, s, here],
            send_sem=r_send.at[c, way, s],
            recv_sem=r_recv.at[c, way, s],
            device_id=z_plus,
            device_id_type=MESH,
        ).wait_recv()
        if c == LEAD:
            degree_copy(way, s, z_plus).wait_recv()

    def finish(c, final):
        arrived = (2, 3) if TREE[c] else (3,)
        for way in range(2):
            for s in arrived:
                ring_got(c, way, s, DEST)
        for b in range(DEST):
            if c == LEAD:
                mine = 1.0 + degree_row(z, b)
                for way in range(2):
                    for s in arrived:
                        mine = mine + deg_recv[way, s, b : b + 1]
                degree[b : b + 1] = mine
            val = partial(c, z, b)
            for way in range(2):
                for s in arrived:
                    val = val + rs_recv[c][way, s, b].astype(F32)
            mean = (val / degree[b : b + 1]).astype(BF16)
            here = pl.ds(b * BLK, BLK)
            total = acc[here, :] + tn(mean, wn_ref[STARTS[c] : STARTS[c] + SIZES[c], :])
            if final:
                out_ref[here, :] = jnp.maximum(total, 0.0).astype(BF16)
            else:
                acc[here, :] = total

    def prepare():
        make_plan()
        own_part()

    run = {
        "own": own_out,
        "ff0": lambda c: first_forward(c, 0),
        "ff1": lambda c: first_forward(c, 1),
        "of0": lambda c: own_forward(c, 0),
        "of1": lambda c: own_forward(c, 1),
        "ro": rest_out,
        "rf0": lambda c: rest_forward(c, 0),
        "rf1": lambda c: rest_forward(c, 1),
        "far": far_in,
        "sib": sibling_in,
    }
    for q in range(PARTS):
        run[f"comp{q}"] = functools.partial(compute, q=q)
    for s in range(HOPS):
        run[f"ring{s}"] = functools.partial(ring, s=s)
    for stage in range(3):
        run[f"t{stage}"] = functools.partial(tree, stage=stage)
    final = [n for n, (name, _) in enumerate(ORDER) if name == "fin"][-1]
    ready = loaded = False
    for n, (name, c) in enumerate(ORDER):
        if name == "comp0" and not loaded:
            tile_load.wait()
            loaded = True
        if name != "own" and not ready:
            prepare()
            ready = True
        if name == "fin":
            finish(c, n == final)
        else:
            run[name](c)

    for copy in sent:
        copy.wait_send()


def per_device(
    features, adjacency, block_rows, block_cols, live_counts, self_weight, neigh_weight, out_bias
):
    vmem = pl.BlockSpec(memory_space=pltpu.VMEM)
    smem = pl.BlockSpec(memory_space=pltpu.SMEM)
    hbm = pl.BlockSpec(memory_space=pltpu.HBM)
    dma = pltpu.SemaphoreType.DMA
    return pl.pallas_call(
        layer_kernel,
        out_shape=pltpu.VMEM((DEST * BLK, HID), BF16),
        in_specs=[smem, vmem, vmem, hbm, hbm, hbm, hbm, hbm],
        out_specs=vmem,
        scratch_shapes=[pltpu.VMEM((2, SIDE, SUB, size, BLK), BF16) for size in SIZES]
        + [pltpu.VMEM((SLOTS + 1, size, BLK), F32) for size in SIZES]
        + [pltpu.VMEM((2, HOPS, DEST, size, BLK), BF16) for size in SIZES]
        + [pltpu.VMEM((2, HOPS, DEST, size, BLK), BF16) for size in SIZES]
        + [
            pltpu.VMEM((SLOTS, BLK, BLK), BF16),
            pltpu.VMEM((SLOTS + 1, 8, BLK), F32),
            pltpu.VMEM((2, HOPS, DEST, BLK), F32),
            pltpu.VMEM((2, HOPS, DEST, BLK), F32),
            pltpu.VMEM((DEST, BLK), F32),
            pltpu.VMEM((DEST * BLK, FEAT), BF16),
            pltpu.VMEM((FEAT, HID), BF16),
            pltpu.VMEM((FEAT, HID), BF16),
            pltpu.VMEM((1, HID), F32),
            pltpu.VMEM((DEST * BLK, HID), F32),
            pltpu.VMEM((8, LANES), I32),
            pltpu.SMEM((8, LANES), I32),
            dma,
            dma((5,)),
            dma((CHUNKS, N_GATHER)),
            dma((CHUNKS, N_GATHER)),
            dma((CHUNKS, 2, HOPS)),
            dma((CHUNKS, 2, HOPS)),
            dma((2, HOPS)),
            dma((2, HOPS)),
        ],
        compiler_params=pltpu.CompilerParams(
            collective_id=0, has_side_effects=True, vmem_limit_bytes=56 * 2**20
        ),
    )(
        live_counts,
        block_rows,
        block_cols,
        features,
        adjacency,
        self_weight,
        neigh_weight,
        out_bias.reshape(1, HID),
    )


def solution(mesh):
    in_specs = (
        P(("row", "col"), None),
        P("row", "col", None, None, None),
        P("row", "col", None),
        P("row", "col", None),
        P("row", "col"),
        P(),
        P(),
        P(),
    )
    out_specs = P(("row", "col"), None)
    return jax.shard_map(
        per_device, mesh=mesh, in_specs=in_specs, out_specs=out_specs, check_vma=False
    )
```
